32 devices in a mesh: gy: 4 (over y, x), gz: 8 (over z, core).
Axes of the slice: x: 2, y: 2, z: 4, core: 2. Of those that a mesh axis runs over, the one named last changes fastest.
Arguments:
- field: bfloat16 [32, 33, 16, 512], P(None, None, 'gz', 'gy'), may hold values from -6 to 6
- weight: bfloat16 [3, 27, 32], replicated, may hold values from -0.5 to 0.5
- bias: float32 [3], replicated, may hold values from -1 to 1
- cotangent: bfloat16 [3, 64, 32, 1024], P(None, None, 'gz', 'gy'), may hold values from -6 to 6
Outputs:
- displacement: bfloat16 [3, 64, 32, 1024], P(None, None, 'gz', 'gy')
- grad_input: bfloat16 [32, 33, 16, 512], P(None, None, 'gz', 'gy')
- grad_weight: float32 [3, 27, 32], replicated
- grad_bias: float32 [3], replicated
The draws below stay inside these ranges and needn't reach their ends.
All inputs are finite; a program needn't handle non-finite values.
Results may differ from the reference program's by a relative error of at most 0.0035.
Values may be sent and summed in bfloat16 or wider, within the bound.
A program may use at most 128 MiB of HBM per device.

```python
import math
import jax
import jax.numpy as jnp
from jax import lax

CIN = 32
COUT = 3
TAPS = 27
XC = 32
NZ = 16
NY = 512


def steps_of(own_key, shape, split, smallest, high):
    def one(axis_at, parts):
        draws = jax.random.uniform(jax.random.fold_in(jax.random.fold_in(own_key, 6), axis_at), (parts,), jnp.float32, smallest / len(split), high / len(split))
        return jnp.repeat(jnp.exp(draws), shape[axis_at] // parts).reshape((-1,) + (1,) * (len(shape) - axis_at - 1))

    level = one(*split[0])
    for cut in split[1:]:
        level = level * one(*cut)
    return level


def centred(own_key, shape, deviation, bound, shards=(), held_as=jnp.bfloat16):
    level = steps_of(own_key, shape, shards, -0.22, 0.18) if shards else 1.0
    drawn = jax.random.normal(own_key, shape, jnp.float32) * deviation * level
    return jnp.minimum(jnp.maximum(drawn, -bound), bound).astype(held_as)


def setup_inputs(seed: int = 0) -> dict:
    seeds = jax.random.split(jax.random.key(seed), 5)
    return {
        "field": centred(seeds[0], (CIN, XC + 1, NZ, NY), 1.0, 6.0, ((2, 8), (3, 4))),
        "weight": centred(seeds[1], (COUT, TAPS, CIN), (CIN * 4) ** -0.5, 0.5),
        "bias": jnp.clip(jax.random.uniform(seeds[2], (COUT,), jnp.float32, -1.0, 1.0), -1.0, 1.0),
        "cotangent": centred(seeds[3], (COUT, 2 * XC, 2 * NZ, 2 * NY), 1.0, 6.0, ((2, 8), (3, 4))),
    }


def alternate(parities):
    by_x = []
    for parity_x in range(2):
        by_z = []
        for parity_z in range(2):
            by_z.append(jnp.stack([parities[parity_x, parity_z, 0], parities[parity_x, parity_z, 1]], axis=-1))
        by_x.append(jnp.stack(by_z, axis=3))
    stacked_all = jnp.stack(by_x, axis=2)
    extent = stacked_all.shape
    return stacked_all.reshape(extent[0], extent[1] * 2, extent[3] * 2, extent[5] * 2)

def reference(field, weight, bias, cotangent):
    flattened = field.reshape(CIN, -1)
    parities = {}
    for kernel in range(27):
        along_x = kernel // 9
        along_y = kernel // 3 % 3
        along_z = kernel % 3
        contribution = jnp.dot(weight[:, kernel, :], flattened, preferred_element_type=jnp.float32)
        contribution = contribution.reshape((COUT, XC + 1, NZ, NY))
        contribution = contribution[:, 1:] if along_x == 0 else contribution[:, :XC]
        if along_z == 0:
            contribution = jnp.roll(contribution, -1, 2)
        if along_y == 0:
            contribution = jnp.roll(contribution, -1, 3)
        parity_key = (0 if along_x == 1 else 1, 0 if along_z == 1 else 1, 0 if along_y == 1 else 1)
        if parity_key in parities:
            parities[parity_key] = parities[parity_key] + contribution
        else:
            parities[parity_key] = contribution
    displacement = (alternate(parities) + bias[:, None, None, None]).astype(jnp.bfloat16)
    extended = jnp.roll(cotangent, 1, 2)
    extended = jnp.concatenate([extended, extended[:, :, :1, :]], axis=2)
    extended = jnp.roll(extended, 1, 3)
    extended = jnp.concatenate([extended, extended[:, :, :, :1]], axis=3)
    extended = jnp.pad(extended, ((0, 0), (1, 2), (0, 0), (0, 0)))
    grad_sum = jnp.zeros((CIN, (XC + 1) * NZ * NY), jnp.float32)
    weight_terms = []
    for kernel in range(27):
        along_x = kernel // 9
        along_y = kernel // 3 % 3
        along_z = kernel % 3
        piece = lax.slice(extended, (0, along_x, along_z, along_y), (COUT, along_x + 2 * XC + 1, along_z + 2 * NZ - 1, along_y + 2 * NY - 1), (1, 2, 2, 2))
        piece_flat = piece.reshape(COUT, -1)
        grad_sum = grad_sum + jnp.dot(weight[:, kernel, :].T, piece_flat, preferred_element_type=jnp.float32)
        weight_terms.append(jnp.dot(piece_flat, flattened.T, preferred_element_type=jnp.float32))
    grad_input = grad_sum.reshape(CIN, XC + 1, NZ, NY).astype(jnp.bfloat16)
    scale = 1.0 / math.sqrt(8 * XC * NZ * NY)
    grad_weight = jnp.stack(weight_terms, axis=1) * scale
    grad_bias = lax.optimization_barrier(jnp.sum(cotangent.astype(jnp.float32), axis=(1, 2, 3))) * scale
    return (displacement, grad_input, grad_weight, grad_bias)
```

```python
import functools
import math

import jax
import jax.numpy as jnp
import numpy as np
from jax import lax
from jax.experimental import pallas as pl
from jax.experimental.pallas import tpu as pltpu
from jax.sharding import PartitionSpec as P

MESH = pl.DeviceIdType.MESH
F32 = jnp.float32
BF16 = jnp.bfloat16
LINK = {1: (0, 0), 2: (1, 0), 0: (1, 1)}


def selectors():
    forward = np.zeros((3, 48, 384), np.float32)
    backward = np.zeros((2, 96, 192), np.float32)
    for o in range(3):
        for t in range(27):
            (px, dx), (py, dy), (pz, dz) = LINK[t // 9], LINK[t // 3 % 3], LINK[t % 3]
            for z in range(2):
                block = dx * 6 + (z + dz) * 2 + dy
                row = py * 24 + o * 8 + px * 4 + z * 2 + pz
                forward[block // 4, row, block % 4 * 96 + o * 32 + t] = 1
                below = z - dz
                line = o * 8 + px * 4 + below * 2 + pz if below >= 0 else 24 + (3 + 4 * px + o) % 8
                backward[z, o * 32 + t, (1 - dx) * 96 + (py + dy) * 32 + line] = 1
    return forward, backward


def dot(a, b):
    return jnp.dot(a, b, preferred_element_type=F32)


def kernel(
    ny, nz, nx, scale,
    f_ref, w_ref, b_ref, c_ref, self_ref, selg_ref,
    d_ref, gi_ref, gw_ref, gb_ref,
    f32s, fb, yf, yf_y, yf_d, eo, hs, hr, yc, yc_y, yc_d, cb, gis, des, wp,
    part, zsum, zrecv, yrecv,
    send_sem, recv_sem, zsend, zrsem, ysend, yrsem,
):
    my, mz = lax.axis_index("gy"), lax.axis_index("gz")
    y_up, y_dn = lax.rem(my + 1, ny), lax.rem(my + ny - 1, ny)
    z_up, z_dn = lax.rem(mz + 1, nz), lax.rem(mz + nz - 1, nz)
    rows = 2 * (nx + 1)

    barrier = pltpu.get_barrier_semaphore()
    for j in range(1, nz):
        pl.semaphore_signal(barrier, inc=1, device_id=(my, lax.rem(mz + j, nz)), device_id_type=MESH)
    for j in range(1, ny):
        pl.semaphore_signal(barrier, inc=1, device_id=(lax.rem(my + j, ny), mz), device_id_type=MESH)
    pl.semaphore_signal(barrier, inc=1, device_id=(y_up, z_up), device_id_type=MESH)
    pl.semaphore_signal(barrier, inc=1, device_id=(y_dn, z_dn), device_id_type=MESH)

    lane = lax.broadcasted_iota(jnp.int32, (32, 128), 1)
    sub = lax.broadcasted_iota(jnp.int32, (8, 128), 0) % 4

    f32s[...] = f_ref[...].astype(F32)

    def field_step(x, column):
        for z in range(2):
            m = f32s[pl.ds(2 * x + z, 32, stride=rows), :]
            fb[x, pl.ds(64 * z, 32), :] = m.astype(BF16)
            column = jnp.where(lane == 64 * z + x, m[:, 0:1], column)
        return column

    yf[...] = lax.fori_loop(0, nx + 1, field_step, jnp.zeros((32, 128), F32)).astype(BF16)

    pl.semaphore_wait(barrier, nz - 1 + ny - 1 + 2)

    def send(k, src, dst, device):
        copy = pltpu.make_async_remote_copy(
            src_ref=src, dst_ref=dst, send_sem=send_sem.at[k], recv_sem=recv_sem.at[k],
            device_id=device, device_id_type=MESH,
        )
        copy.start()
        return copy

    f_copies = [
        send(0, fb.at[:, pl.ds(0, 32), :], fb.at[:, pl.ds(128, 32), :], (my, z_dn)),
        send(1, yf, yf_y, (y_dn, mz)),
        send(2, yf, yf_d, (y_dn, z_dn)),
    ]

    i0 = lax.broadcasted_iota(jnp.int32, (256, 256), 0)
    i1 = lax.broadcasted_iota(jnp.int32, (256, 256), 1)
    split = jnp.where(i0 == 2 * (i1 % 128) + i1 // 128, 1.0, 0.0).astype(BF16)
    join = jnp.where(i1 == 2 * (i0 % 128) + i0 // 128, 1.0, 0.0).astype(BF16)
    eo[...] = dot(c_ref[...], split)

    def parts_of(x, half):
        return [
            eo[pl.ds(pl.multiple_of(o * 8 * nx + x * 8, 8), 8), 128 * half:128 * half + 128]
            for o in range(3)
        ]

    def last_z(p):
        top = jnp.where(sub == 3, p[0], 0.0)
        top = jnp.where(sub == 0, pltpu.roll(p[1], 1, 0), top)
        return jnp.where(sub == 1, pltpu.roll(p[2], 2, 0), top)

    def cot_step(x, carry):
        column, sums = carry
        even, odd = parts_of(x, 0), parts_of(x, 1)
        h_even, h_odd = last_z(even), last_z(odd)
        hs[x] = jnp.concatenate([h_even, h_odd], axis=0).astype(BF16)
        m = jnp.concatenate(odd + [h_odd], axis=0)
        column = jnp.where(lane == x, m[:, 127:128], column)
        sums = [s + e + q for s, e, q in zip(sums, even, odd)]
        return column, sums

    zero8 = jnp.zeros((8, 128), F32)
    column, sums = lax.fori_loop(
        0, nx, cot_step, (jnp.zeros((32, 128), F32), [zero8, zero8, zero8])
    )
    yc[...] = column.astype(BF16)
    c_copies = [
        send(3, hs, hr, (my, z_up)),
        send(4, yc, yc_y, (y_up, mz)),
        send(5, yc, yc_d, (y_up, z_up)),
    ]

    wp[...] = jnp.zeros_like(wp)
    for o in range(3):
        wp[32 * o:32 * o + 27, 0:32] = w_ref[o].astype(F32)
    wv = wp[...]
    wt = wv + pltpu.roll(wv, 32, 1) + pltpu.roll(wv, 64, 1) + pltpu.roll(wv, 96, 1)
    lane96 = lax.broadcasted_iota(jnp.int32, (96, 128), 1) // 32
    stacked = jnp.concatenate([jnp.where(lane96 == g, wt, 0.0) for g in range(4)], axis=0).astype(BF16)
    w_fwd = jnp.concatenate([dot(self_ref[j], stacked) for j in range(3)], axis=1).astype(BF16)
    w_t = wv.T[0:32].astype(BF16)
    w_bwd = jnp.concatenate([dot(w_t, selg_ref[z]) for z in range(2)], axis=0).astype(BF16)

    for copy in c_copies:
        copy.wait()

    cb[0] = jnp.zeros((96, 128), BF16)
    cb[nx + 1] = jnp.zeros((96, 128), BF16)
    edge = jnp.concatenate([yc_y[...].astype(F32)[0:24], yc_d[...].astype(F32)[24:32]], axis=0)

    def widen_cot(x, _):
        below = hr[x].astype(F32)
        even = jnp.concatenate(parts_of(x, 0) + [below[0:8]], axis=0)
        odd = jnp.concatenate(parts_of(x, 1) + [below[8:16]], axis=0)
        first = pltpu.roll(edge, 128 - x, 1)
        moved = jnp.where(lane == 0, first, pltpu.roll(odd, 1, 1))
        cb[x + 1] = jnp.concatenate([even, odd, moved], axis=0).astype(BF16)
        return 0

    lax.fori_loop(0, nx, widen_cot, 0)

    def backward(x, acc):
        taps = cb[pl.ds(x, 2)].reshape(192, 128)
        g = dot(w_bwd, taps)
        gis[pl.ds(2 * x, 32, stride=rows), :] = g[0:32]
        gis[pl.ds(2 * x + 1, 32, stride=rows), :] = g[32:64]
        f0, f1 = fb[x, pl.ds(0, 32), :], fb[x, pl.ds(64, 32), :]
        ff = jnp.concatenate([f0, f1, f0, f1], axis=0)
        return acc + lax.dot_general(taps, ff, (((1,), (1,)), ((), ())), preferred_element_type=F32)

    acc = lax.fori_loop(0, nx + 1, backward, jnp.zeros((192, 128), F32))
    hi = acc.astype(BF16)
    lo = (acc - hi.astype(F32)).astype(BF16)
    v0 = dot(selg_ref[0], hi) + dot(selg_ref[0], lo)
    v1 = dot(selg_ref[1], hi) + dot(selg_ref[1], lo)
    g = v0 + pltpu.roll(v1, 96, 1)
    packed = jnp.where(
        lane < 32, g[0:32],
        jnp.where(lane < 64, pltpu.roll(g[32:64], 32, 1), pltpu.roll(g[64:96], 64, 1)),
    )
    for o in range(3):
        packed = jnp.where(lane == 96 + o, jnp.sum(sums[o]), packed)
    part[...] = packed
    zrecv[mz] = packed
    z_copies = []
    for j in range(1, nz):
        copy = pltpu.make_async_remote_copy(
            src_ref=part, dst_ref=zrecv.at[mz], send_sem=zsend.at[j - 1], recv_sem=zrsem.at[j - 1],
            device_id=(my, lax.rem(mz + j, nz)), device_id_type=MESH,
        )
        copy.start()
        z_copies.append(copy)

    for copy in f_copies:
        copy.wait()

    edge_y = yf_y[...].astype(F32)
    edge_d = yf_d[...].astype(F32)

    def widen_field(x, _):
        for z in range(3):
            m = fb[x, pl.ds(64 * z, 32), :].astype(F32)
            source, at = (edge_y, 64 * z) if z < 2 else (edge_d, 0)
            last = pltpu.roll(source, 127 - at - x, 1)
            moved = jnp.where(lane == 127, last, pltpu.roll(m, 127, 1))
            fb[x, pl.ds(64 * z + 32, 32), :] = moved.astype(BF16)
        return 0

    lax.fori_loop(0, nx + 1, widen_field, 0)

    def forward(x, _):
        taps = fb[pl.ds(x, 2)].reshape(384, 128)
        d = dot(w_fwd, taps)
        for half in range(2):
            for o in range(3):
                at = 24 * half + 8 * o
                row = pl.multiple_of(o * 8 * nx + x * 8, 8)
                des[pl.ds(row, 8), 128 * half:128 * half + 128] = d[at:at + 8] + b_ref[o]
        return 0

    lax.fori_loop(0, nx, forward, 0)

    for copy in z_copies:
        copy.wait()
    total = zrecv[0]
    for j in range(1, nz):
        total = total + zrecv[j]
    zsum[...] = total
    yrecv[my] = total
    y_copies = []
    for j in range(1, ny):
        copy = pltpu.make_async_remote_copy(
            src_ref=zsum, dst_ref=yrecv.at[my], send_sem=ysend.at[j - 1], recv_sem=yrsem.at[j - 1],
            device_id=(lax.rem(my + j, ny), mz), device_id_type=MESH,
        )
        copy.start()
        y_copies.append(copy)

    gi_ref[...] = gis[...].astype(BF16)
    d_ref[...] = dot(des[...].astype(BF16), join).astype(BF16)

    for copy in y_copies:
        copy.wait()
    total = yrecv[0]
    for j in range(1, ny):
        total = total + yrecv[j]
    total = total * scale
    for o in range(3):
        gw_ref[o] = (total if o == 0 else pltpu.roll(total, 128 - 32 * o, 1))[0:27, 0:32]
        gb_ref[o] = jnp.sum(jnp.where(lane[0:1] == 96 + o, total[0:1], 0.0))


def body(ny, nz, field, weight, bias, cotangent):
    channels, planes, depth, width = field.shape
    nx = planes - 1
    cells = 8 * nx * depth * width * ny * nz
    forward, backward = selectors()
    fine = cotangent.shape
    vmem = pl.BlockSpec(memory_space=pltpu.VMEM)
    smem = pl.BlockSpec(memory_space=pltpu.SMEM)
    n_f, n_c = channels * planes * depth, fine[0] * fine[1] * fine[2]
    d, gi, gw, gb = pl.pallas_call(
        functools.partial(kernel, ny, nz, nx, 1.0 / math.sqrt(cells)),
        out_shape=(
            jax.ShapeDtypeStruct((n_c, fine[3]), BF16),
            jax.ShapeDtypeStruct((n_f, width), BF16),
            jax.ShapeDtypeStruct(weight.shape, F32),
            jax.ShapeDtypeStruct(bias.shape, F32),
        ),
        in_specs=[vmem, vmem, smem, vmem, vmem, vmem],
        out_specs=(vmem, vmem, vmem, smem),
        scratch_shapes=[
            pltpu.VMEM((n_f, 128), F32),
            pltpu.VMEM((nx + 1, 192, 128), BF16),
            pltpu.VMEM((32, 128), BF16),
            pltpu.VMEM((32, 128), BF16),
            pltpu.VMEM((32, 128), BF16),
            pltpu.VMEM((n_c, 256), F32),
            pltpu.VMEM((nx, 16, 128), BF16),
            pltpu.VMEM((nx, 16, 128), BF16),
            pltpu.VMEM((32, 128), BF16),
            pltpu.VMEM((32, 128), BF16),
            pltpu.VMEM((32, 128), BF16),
            pltpu.VMEM((nx + 2, 96, 128), BF16),
            pltpu.VMEM((n_f, 128), F32),
            pltpu.VMEM((n_c, 256), F32),
            pltpu.VMEM((96, 128), F32),
            pltpu.VMEM((32, 128), F32),
            pltpu.VMEM((32, 128), F32),
            pltpu.VMEM((nz, 32, 128), F32),
            pltpu.VMEM((ny, 32, 128), F32),
            pltpu.SemaphoreType.DMA((6,)),
            pltpu.SemaphoreType.DMA((6,)),
            pltpu.SemaphoreType.DMA((nz - 1,)),
            pltpu.SemaphoreType.DMA((nz - 1,)),
            pltpu.SemaphoreType.DMA((ny - 1,)),
            pltpu.SemaphoreType.DMA((ny - 1,)),
        ],
        compiler_params=pltpu.CompilerParams(
            collective_id=0, has_side_effects=True, vmem_limit_bytes=32 * 1024 * 1024
        ),
    )(
        field.reshape(n_f, width), weight, bias, cotangent.reshape(n_c, fine[3]),
        jnp.asarray(forward, BF16), jnp.asarray(backward, BF16),
    )
    return d.reshape(fine), gi.reshape(field.shape), gw, gb


def solution(mesh):
    return jax.shard_map(
        functools.partial(body, mesh.shape["gy"], mesh.shape["gz"]),
        mesh=mesh,
        in_specs=(P(None, None, "gz", "gy"), P(), P(), P(None, None, "gz", "gy")),
        out_specs=(P(None, None, "gz", "gy"), P(None, None, "gz", "gy"), P(), P()),
        check_vma=False,
    )
```

```python
import functools
import math

import jax
import jax.numpy as jnp
import numpy as np
from jax import lax
from jax.experimental import pallas as pl
from jax.experimental.pallas import tpu as pltpu
from jax.sharding import PartitionSpec as P

MESH = pl.DeviceIdType.MESH
F32 = jnp.float32
BF16 = jnp.bfloat16
LINK = {1: (0, 0), 2: (1, 0), 0: (1, 1)}


def selectors():
    forward = np.zeros((3, 48, 384), np.float32)
    backward = np.zeros((2, 96, 192), np.float32)
    for o in range(3):
        for t in range(27):
            (px, dx), (py, dy), (pz, dz) = LINK[t // 9], LINK[t // 3 % 3], LINK[t % 3]
            for z in range(2):
                block = dx * 6 + (z + dz) * 2 + dy
                row = py * 24 + o * 8 + px * 4 + z * 2 + pz
                forward[block // 4, row, block % 4 * 96 + o * 32 + t] = 1
                below = z - dz
                line = o * 8 + px * 4 + below * 2 + pz if below >= 0 else 24 + (3 + 4 * px + o) % 8
                backward[z, o * 32 + t, (1 - dx) * 96 + (py + dy) * 32 + line] = 1
    return forward, backward


def dot(a, b):
    return jnp.dot(a, b, preferred_element_type=F32)


def in_blocks(count, step, carry, most=11):
    size = max(k for k in range(1, most + 1) if count % k == 0)

    def block(i, carry):
        stores = []
        for k in range(size):
            carry, more = step(i * size + k, carry)
            stores += more
        for ref, index, value in stores:
            ref[index] = value
        return carry

    return lax.fori_loop(0, count // size, block, carry)


def kernel(
    ny, nz, nx, scale,
    f_ref, w_ref, b_ref, c_ref, self_ref, selg_ref,
    d_ref, gi_ref, gw_ref, gb_ref,
    f32s, fb, yf, yf_y, yf_d, eo, hs, hr, yc, yc_y, yc_d, cb, gis, des, wp,
    part, zsum, zrecv, yrecv,
    send_sem, recv_sem, zsend, zrsem, ysend, yrsem,
):
    my, mz = lax.axis_index("gy"), lax.axis_index("gz")
    y_up, y_dn = lax.rem(my + 1, ny), lax.rem(my + ny - 1, ny)
    z_up, z_dn = lax.rem(mz + 1, nz), lax.rem(mz + nz - 1, nz)
    rows = 2 * (nx + 1)

    barrier = pltpu.get_barrier_semaphore()
    for j in range(1, nz):
        pl.semaphore_signal(barrier, inc=1, device_id=(my, lax.rem(mz + j, nz)), device_id_type=MESH)
    for j in range(1, ny):
        pl.semaphore_signal(barrier, inc=1, device_id=(lax.rem(my + j, ny), mz), device_id_type=MESH)
    pl.semaphore_signal(barrier, inc=1, device_id=(y_up, z_up), device_id_type=MESH)
    pl.semaphore_signal(barrier, inc=1, device_id=(y_dn, z_dn), device_id_type=MESH)

    lane = lax.broadcasted_iota(jnp.int32, (32, 128), 1)
    sub = lax.broadcasted_iota(jnp.int32, (8, 128), 0) % 4

    f32s[...] = f_ref[...].astype(F32)

    def field_step(x, column):
        stores = []
        for z in range(2):
            m = f32s[pl.ds(2 * x + z, 32, stride=rows), :]
            stores.append((fb, (x, pl.ds(64 * z, 32)), m.astype(BF16)))
            column = jnp.where(lane == 64 * z + x, m[:, 0:1], column)
        return column, stores

    yf[...] = in_blocks(nx + 1, field_step, jnp.zeros((32, 128), F32)).astype(BF16)

    pl.semaphore_wait(barrier, nz - 1 + ny - 1 + 2)

    def send(k, src, dst, device):
        copy = pltpu.make_async_remote_copy(
            src_ref=src, dst_ref=dst, send_sem=send_sem.at[k], recv_sem=recv_sem.at[k],
            device_id=device, device_id_type=MESH,
        )
        copy.start()
        return copy

    f_copies = [
        send(0, fb.at[:, pl.ds(0, 32), :], fb.at[:, pl.ds(128, 32), :], (my, z_dn)),
        send(1, yf, yf_y, (y_dn, mz)),
        send(2, yf, yf_d, (y_dn, z_dn)),
    ]

    i0 = lax.broadcasted_iota(jnp.int32, (256, 256), 0)
    i1 = lax.broadcasted_iota(jnp.int32, (256, 256), 1)
    split = jnp.where(i0 == 2 * (i1 % 128) + i1 // 128, 1.0, 0.0).astype(BF16)
    join = jnp.where(i1 == 2 * (i0 % 128) + i0 // 128, 1.0, 0.0).astype(BF16)
    eo[...] = dot(c_ref[...], split)

    def parts_of(x, half):
        return [
            eo[pl.ds(pl.multiple_of(o * 8 * nx + x * 8, 8), 8), 128 * half:128 * half + 128]
            for o in range(3)
        ]

    def last_z(p):
        top = jnp.where(sub == 3, p[0], 0.0)
        top = jnp.where(sub == 0, pltpu.roll(p[1], 1, 0), top)
        return jnp.where(sub == 1, pltpu.roll(p[2], 2, 0), top)

    def cot_step(x, carry):
        column, sums = carry
        even, odd = parts_of(x, 0), parts_of(x, 1)
        h_even, h_odd = last_z(even), last_z(odd)
        halo = jnp.concatenate([h_even, h_odd], axis=0).astype(BF16)
        m = jnp.concatenate(odd + [h_odd], axis=0)
        column = jnp.where(lane == x, m[:, 127:128], column)
        sums = [s + e + q for s, e, q in zip(sums, even, odd)]
        return (column, sums), [(hs, x, halo)]

    zero8 = jnp.zeros((8, 128), F32)
    column, sums = in_blocks(
        nx, cot_step, (jnp.zeros((32, 128), F32), [zero8, zero8, zero8])
    )
    yc[...] = column.astype(BF16)
    c_copies = [
        send(3, hs, hr, (my, z_up)),
        send(4, yc, yc_y, (y_up, mz)),
        send(5, yc, yc_d, (y_up, z_up)),
    ]

    wp[...] = jnp.zeros_like(wp)
    for o in range(3):
        wp[32 * o:32 * o + 27, 0:32] = w_ref[o].astype(F32)
    wv = wp[...]
    wt = wv + pltpu.roll(wv, 32, 1) + pltpu.roll(wv, 64, 1) + pltpu.roll(wv, 96, 1)
    lane96 = lax.broadcasted_iota(jnp.int32, (96, 128), 1) // 32
    stacked = jnp.concatenate([jnp.where(lane96 == g, wt, 0.0) for g in range(4)], axis=0).astype(BF16)
    w_fwd = jnp.concatenate([dot(self_ref[j], stacked) for j in range(3)], axis=1).astype(BF16)
    w_t = wv.T[0:32].astype(BF16)
    w_bwd = jnp.concatenate([dot(w_t, selg_ref[z]) for z in range(2)], axis=0).astype(BF16)

    for copy in c_copies:
        copy.wait()

    cb[0] = jnp.zeros((96, 128), BF16)
    cb[nx + 1] = jnp.zeros((96, 128), BF16)
    edge = jnp.concatenate([yc_y[...].astype(F32)[0:24], yc_d[...].astype(F32)[24:32]], axis=0)

    def widen_cot(x, _):
        below = hr[x].astype(F32)
        even = jnp.concatenate(parts_of(x, 0) + [below[0:8]], axis=0)
        odd = jnp.concatenate(parts_of(x, 1) + [below[8:16]], axis=0)
        first = pltpu.roll(edge, 128 - x, 1)
        moved = jnp.where(lane == 0, first, pltpu.roll(odd, 1, 1))
        return 0, [(cb, x + 1, jnp.concatenate([even, odd, moved], axis=0).astype(BF16))]

    in_blocks(nx, widen_cot, 0)

    def backward(x, acc):
        taps = cb[pl.ds(x, 2)].reshape(192, 128)
        g = dot(w_bwd, taps)
        stores = [(gis, pl.ds(2 * x + z, 32, stride=rows), g[32 * z:32 * z + 32]) for z in range(2)]
        f0, f1 = fb[x, pl.ds(0, 32), :], fb[x, pl.ds(64, 32), :]
        ff = jnp.concatenate([f0, f1, f0, f1], axis=0)
        acc = acc + lax.dot_general(taps, ff, (((1,), (1,)), ((), ())), preferred_element_type=F32)
        return acc, stores

    acc = in_blocks(nx + 1, backward, jnp.zeros((192, 128), F32))
    hi = acc.astype(BF16)
    lo = (acc - hi.astype(F32)).astype(BF16)
    v0 = dot(selg_ref[0], hi) + dot(selg_ref[0], lo)
    v1 = dot(selg_ref[1], hi) + dot(selg_ref[1], lo)
    g = v0 + pltpu.roll(v1, 96, 1)
    packed = jnp.where(
        lane < 32, g[0:32],
        jnp.where(lane < 64, pltpu.roll(g[32:64], 32, 1), pltpu.roll(g[64:96], 64, 1)),
    )
    for o in range(3):
        packed = jnp.where(lane == 96 + o, jnp.sum(sums[o]), packed)
    part[...] = packed
    zrecv[mz] = packed
    z_copies = []
    for j in range(1, nz):
        copy = pltpu.make_async_remote_copy(
            src_ref=part, dst_ref=zrecv.at[mz], send_sem=zsend.at[j - 1], recv_sem=zrsem.at[j - 1],
            device_id=(my, lax.rem(mz + j, nz)), device_id_type=MESH,
        )
        copy.start()
        z_copies.append(copy)

    for copy in f_copies:
        copy.wait()

    edge_y = yf_y[...].astype(F32)
    edge_d = yf_d[...].astype(F32)

    def widen_field(x, _):
        stores = []
        for z in range(3):
            m = fb[x, pl.ds(64 * z, 32), :].astype(F32)
            source, at = (edge_y, 64 * z) if z < 2 else (edge_d, 0)
            last = pltpu.roll(source, 127 - at - x, 1)
            moved = jnp.where(lane == 127, last, pltpu.roll(m, 127, 1))
            stores.append((fb, (x, pl.ds(64 * z + 32, 32)), moved.astype(BF16)))
        return 0, stores

    in_blocks(nx + 1, widen_field, 0)

    def forward(x, _):
        taps = fb[pl.ds(x, 2)].reshape(384, 128)
        d = dot(w_fwd, taps)
        stores = []
        for half in range(2):
            for o in range(3):
                at = 24 * half + 8 * o
                row = pl.multiple_of(o * 8 * nx + x * 8, 8)
                index = (pl.ds(row, 8), pl.ds(128 * half, 128))
                stores.append((des, index, d[at:at + 8] + b_ref[o]))
        return 0, stores

    in_blocks(nx, forward, 0)

    for copy in z_copies:
        copy.wait()
    total = zrecv[0]
    for j in range(1, nz):
        total = total + zrecv[j]
    zsum[...] = total
    yrecv[my] = total
    y_copies = []
    for j in range(1, ny):
        copy = pltpu.make_async_remote_copy(
            src_ref=zsum, dst_ref=yrecv.at[my], send_sem=ysend.at[j - 1], recv_sem=yrsem.at[j - 1],
            device_id=(lax.rem(my + j, ny), mz), device_id_type=MESH,
        )
        copy.start()
        y_copies.append(copy)

    gi_ref[...] = gis[...].astype(BF16)
    d_ref[...] = dot(des[...].astype(BF16), join).astype(BF16)

    for copy in y_copies:
        copy.wait()
    total = yrecv[0]
    for j in range(1, ny):
        total = total + yrecv[j]
    total = total * scale
    for o in range(3):
        gw_ref[o] = (total if o == 0 else pltpu.roll(total, 128 - 32 * o, 1))[0:27, 0:32]
        gb_ref[o] = jnp.sum(jnp.where(lane[0:1] == 96 + o, total[0:1], 0.0))


def body(ny, nz, field, weight, bias, cotangent):
    channels, planes, depth, width = field.shape
    nx = planes - 1
    cells = 8 * nx * depth * width * ny * nz
    forward, backward = selectors()
    fine = cotangent.shape
    vmem = pl.BlockSpec(memory_space=pltpu.VMEM)
    smem = pl.BlockSpec(memory_space=pltpu.SMEM)
    n_f, n_c = channels * planes * depth, fine[0] * fine[1] * fine[2]
    d, gi, gw, gb = pl.pallas_call(
        functools.partial(kernel, ny, nz, nx, 1.0 / math.sqrt(cells)),
        out_shape=(
            jax.ShapeDtypeStruct((n_c, fine[3]), BF16),
            jax.ShapeDtypeStruct((n_f, width), BF16),
            jax.ShapeDtypeStruct(weight.shape, F32),
            jax.ShapeDtypeStruct(bias.shape, F32),
        ),
        in_specs=[vmem, vmem, smem, vmem, vmem, vmem],
        out_specs=(vmem, vmem, vmem, smem),
        scratch_shapes=[
            pltpu.VMEM((n_f, 128), F32),
            pltpu.VMEM((nx + 1, 192, 128), BF16),
            pltpu.VMEM((32, 128), BF16),
            pltpu.VMEM((32, 128), BF16),
            pltpu.VMEM((32, 128), BF16),
            pltpu.VMEM((n_c, 256), F32),
            pltpu.VMEM((nx, 16, 128), BF16),
            pltpu.VMEM((nx, 16, 128), BF16),
            pltpu.VMEM((32, 128), BF16),
            pltpu.VMEM((32, 128), BF16),
            pltpu.VMEM((32, 128), BF16),
            pltpu.VMEM((nx + 2, 96, 128), BF16),
            pltpu.VMEM((n_f, 128), F32),
            pltpu.VMEM((n_c, 256), F32),
            pltpu.VMEM((96, 128), F32),
            pltpu.VMEM((32, 128), F32),
            pltpu.VMEM((32, 128), F32),
            pltpu.VMEM((nz, 32, 128), F32),
            pltpu.VMEM((ny, 32, 128), F32),
            pltpu.SemaphoreType.DMA((6,)),
            pltpu.SemaphoreType.DMA((6,)),
            pltpu.SemaphoreType.DMA((nz - 1,)),
            pltpu.SemaphoreType.DMA((nz - 1,)),
            pltpu.SemaphoreType.DMA((ny - 1,)),
            pltpu.SemaphoreType.DMA((ny - 1,)),
        ],
        compiler_params=pltpu.CompilerParams(
            collective_id=0, has_side_effects=True, vmem_limit_bytes=32 * 1024 * 1024
        ),
    )(
        field.reshape(n_f, width), weight, bias, cotangent.reshape(n_c, fine[3]),
        jnp.asarray(forward, BF16), jnp.asarray(backward, BF16),
    )
    return d.reshape(fine), gi.reshape(field.shape), gw, gb


def solution(mesh):
    return jax.shard_map(
        functools.partial(body, mesh.shape["gy"], mesh.shape["gz"]),
        mesh=mesh,
        in_specs=(P(None, None, "gz", "gy"), P(), P(), P(None, None, "gz", "gy")),
        out_specs=(P(None, None, "gz", "gy"), P(None, None, "gz", "gy"), P(), P()),
        check_vma=False,
    )
```

```python
import functools
import math

import jax
import jax.numpy as jnp
import numpy as np
from jax import lax
from jax.experimental import pallas as pl
from jax.experimental.pallas import tpu as pltpu
from jax.sharding import PartitionSpec as P

MESH = pl.DeviceIdType.MESH
F32 = jnp.float32
BF16 = jnp.bfloat16
NT = (((1,), (1,)), ((), ()))
LINK = {1: (0, 0), 2: (1, 0), 0: (1, 1)}


def selectors():
    forward = np.zeros((3, 48, 384), np.float32)
    backward = np.zeros((2, 96, 192), np.float32)
    for o in range(3):
        for t in range(27):
            (px, dx), (py, dy), (pz, dz) = LINK[t // 9], LINK[t // 3 % 3], LINK[t % 3]
            for z in range(2):
                block = dx * 6 + (z + dz) * 2 + dy
                row = py * 24 + o * 8 + px * 4 + z * 2 + pz
                forward[block // 4, row, block % 4 * 96 + o * 32 + t] = 1
                below = z - dz
                line = o * 8 + px * 4 + below * 2 + pz if below >= 0 else 24 + (3 + 4 * px + o) % 8
                backward[z, o * 32 + t, (1 - dx) * 96 + (py + dy) * 32 + line] = 1
    return forward, backward


def dot(a, b):
    return jnp.dot(a, b, preferred_element_type=F32)


def in_blocks(count, step, carry, wide=1, most=11):
    size = max(k for k in range(1, most + 1) if count % k == 0)

    def block(i, carry):
        stores = []
        for k in range(0, size, wide):
            xs = [i * size + j for j in range(k, min(k + wide, size))]
            carry, more = step(xs if wide > 1 else xs[0], carry)
            stores += more
        for ref, index, value in stores:
            ref[index] = value
        return carry

    return lax.fori_loop(0, count // size, block, carry)


def kernel(
    ny, nz, nx, scale,
    f_ref, w_ref, b_ref, c_ref, self_ref, selg_ref,
    d_ref, gi_ref, gw_ref, gb_ref,
    f32s, fb, yf, yf_y, yf_d, eo, hs, hr, yc, yc_y, yc_d, cb, gis, des, wp,
    part, zsum, zrecv, yrecv,
    send_sem, recv_sem, zsend, zrsem, ysend, yrsem,
):
    my, mz = lax.axis_index("gy"), lax.axis_index("gz")
    y_up, y_dn = lax.rem(my + 1, ny), lax.rem(my + ny - 1, ny)
    z_up, z_dn = lax.rem(mz + 1, nz), lax.rem(mz + nz - 1, nz)
    rows = 2 * (nx + 1)

    barrier = pltpu.get_barrier_semaphore()
    for j in range(1, nz):
        pl.semaphore_signal(barrier, inc=1, device_id=(my, lax.rem(mz + j, nz)), device_id_type=MESH)
    for j in range(1, ny):
        pl.semaphore_signal(barrier, inc=1, device_id=(lax.rem(my + j, ny), mz), device_id_type=MESH)
    pl.semaphore_signal(barrier, inc=1, device_id=(y_up, z_up), device_id_type=MESH)
    pl.semaphore_signal(barrier, inc=1, device_id=(y_dn, z_dn), device_id_type=MESH)

    lane = lax.broadcasted_iota(jnp.int32, (32, 128), 1)
    sub = lax.broadcasted_iota(jnp.int32, (8, 128), 0) % 4

    def send(k, src, dst, device):
        copy = pltpu.make_async_remote_copy(
            src_ref=src, dst_ref=dst, send_sem=send_sem.at[k], recv_sem=recv_sem.at[k],
            device_id=device, device_id_type=MESH,
        )
        copy.start()
        return copy

    i0 = lax.broadcasted_iota(jnp.int32, (256, 256), 0)
    i1 = lax.broadcasted_iota(jnp.int32, (256, 256), 1)
    split = jnp.where(i0 == 2 * (i1 % 128) + i1 // 128, 1.0, 0.0).astype(BF16)
    join = jnp.where(i1 == 2 * (i0 % 128) + i0 // 128, 1.0, 0.0).astype(BF16)
    eo[...] = dot(c_ref[...], split)

    def parts_of(x, half):
        return [
            eo[pl.ds(pl.multiple_of(o * 8 * nx + x * 8, 8), 8), 128 * half:128 * half + 128]
            for o in range(3)
        ]

    def last_z(p):
        top = jnp.where(sub == 3, p[0], 0.0)
        top = jnp.where(sub == 0, pltpu.roll(p[1], 1, 0), top)
        return jnp.where(sub == 1, pltpu.roll(p[2], 2, 0), top)

    def cot_step(x, carry):
        column, sums = carry
        even, odd = parts_of(x, 0), parts_of(x, 1)
        h_even, h_odd = last_z(even), last_z(odd)
        halo = jnp.concatenate([h_even, h_odd], axis=0).astype(BF16)
        m = jnp.concatenate(odd + [h_odd], axis=0)
        column = jnp.where(lane == x, m[:, 127:128], column)
        sums = [s + e + q for s, e, q in zip(sums, even, odd)]
        return (column, sums), [(hs, x, halo)]

    zero8 = jnp.zeros((8, 128), F32)
    column, sums = in_blocks(
        nx, cot_step, (jnp.zeros((32, 128), F32), [zero8, zero8, zero8])
    )
    yc[...] = column.astype(BF16)
    pl.semaphore_wait(barrier, nz - 1 + ny - 1 + 2)

    c_copies = [
        send(3, hs, hr, (my, z_up)),
        send(4, yc, yc_y, (y_up, mz)),
        send(5, yc, yc_d, (y_up, z_up)),
    ]

    f32s[...] = f_ref[...].astype(F32)

    def field_step(x, column):
        stores = []
        for z in range(2):
            m = f32s[pl.ds(2 * x + z, 32, stride=rows), :]
            stores.append((fb, (x, pl.ds(64 * z, 32)), m.astype(BF16)))
            column = jnp.where(lane == 64 * z + x, m[:, 0:1], column)
        return column, stores

    yf[...] = in_blocks(nx + 1, field_step, jnp.zeros((32, 128), F32)).astype(BF16)

    f_copies = [
        send(0, fb.at[:, pl.ds(0, 32), :], fb.at[:, pl.ds(128, 32), :], (my, z_dn)),
        send(1, yf, yf_y, (y_dn, mz)),
        send(2, yf, yf_d, (y_dn, z_dn)),
    ]

    wp[...] = jnp.zeros_like(wp)
    for o in range(3):
        wp[32 * o:32 * o + 27, 0:32] = w_ref[o].astype(F32)
    wv = wp[...]
    wt = wv + pltpu.roll(wv, 32, 1) + pltpu.roll(wv, 64, 1) + pltpu.roll(wv, 96, 1)
    lane96 = lax.broadcasted_iota(jnp.int32, (96, 128), 1) // 32
    stacked = jnp.concatenate([jnp.where(lane96 == g, wt, 0.0) for g in range(4)], axis=0).astype(BF16)
    w_fwd = jnp.concatenate([dot(self_ref[j], stacked) for j in range(3)], axis=1).astype(BF16)
    w_t = wv.T[0:32].astype(BF16)
    w_bwd = jnp.concatenate([dot(w_t, selg_ref[z]) for z in range(2)], axis=0).astype(BF16)

    for copy in c_copies:
        copy.wait()

    cb[0] = jnp.zeros((96, 128), BF16)
    cb[nx + 1] = jnp.zeros((96, 128), BF16)
    edge = jnp.concatenate([yc_y[...].astype(F32)[0:24], yc_d[...].astype(F32)[24:32]], axis=0)

    def widen_cot(x, _):
        below = hr[x].astype(F32)
        even = jnp.concatenate(parts_of(x, 0) + [below[0:8]], axis=0)
        odd = jnp.concatenate(parts_of(x, 1) + [below[8:16]], axis=0)
        first = pltpu.roll(edge, 128 - x, 1)
        moved = jnp.where(lane == 0, first, pltpu.roll(odd, 1, 1))
        return 0, [(cb, x + 1, jnp.concatenate([even, odd, moved], axis=0).astype(BF16))]

    in_blocks(nx, widen_cot, 0)

    def weight_step(xs, acc):
        taps = jnp.concatenate([cb[pl.ds(x, 2)].reshape(192, 128) for x in xs], axis=1)
        cells = jnp.concatenate([
            jnp.concatenate([fb[x, pl.ds(0, 32), :], fb[x, pl.ds(64, 32), :]], axis=0) for x in xs
        ], axis=1)
        return acc + lax.dot_general(cells, taps, NT, preferred_element_type=F32), []

    acc = in_blocks(nx + 1, weight_step, jnp.zeros((64, 192), F32), 2)
    acc = jnp.concatenate([acc, acc], axis=0)
    hi = acc.astype(BF16)
    lo = (acc - hi.astype(F32)).astype(BF16)
    v0, v1 = [
        lax.dot_general(selg_ref[z], hi, NT, preferred_element_type=F32)
        + lax.dot_general(selg_ref[z], lo, NT, preferred_element_type=F32)
        for z in range(2)
    ]
    g = v0 + pltpu.roll(v1, 96, 1)
    packed = jnp.where(
        lane < 32, g[0:32],
        jnp.where(lane < 64, pltpu.roll(g[32:64], 32, 1), pltpu.roll(g[64:96], 64, 1)),
    )
    for o in range(3):
        packed = jnp.where(lane == 96 + o, jnp.sum(sums[o]), packed)
    part[...] = packed
    zrecv[mz] = packed
    z_copies = []
    for j in range(1, nz):
        copy = pltpu.make_async_remote_copy(
            src_ref=part, dst_ref=zrecv.at[mz], send_sem=zsend.at[j - 1], recv_sem=zrsem.at[j - 1],
            device_id=(my, lax.rem(mz + j, nz)), device_id_type=MESH,
        )
        copy.start()
        z_copies.append(copy)

    def backward(xs, _):
        taps = jnp.concatenate([cb[pl.ds(x, 2)].reshape(192, 128) for x in xs], axis=1)
        g = dot(w_bwd, taps)
        return 0, [
            (gis, pl.ds(2 * x + z, 32, stride=rows), g[32 * z:32 * z + 32, 128 * k:128 * k + 128])
            for k, x in enumerate(xs) for z in range(2)
        ]

    in_blocks(nx + 1, backward, 0, 2)
    gi_ref[...] = gis[...].astype(BF16)

    for copy in z_copies:
        copy.wait()
    total = zrecv[0]
    for j in range(1, nz):
        total = total + zrecv[j]
    zsum[...] = total
    yrecv[my] = total
    y_copies = []
    for j in range(1, ny):
        copy = pltpu.make_async_remote_copy(
            src_ref=zsum, dst_ref=yrecv.at[my], send_sem=ysend.at[j - 1], recv_sem=yrsem.at[j - 1],
            device_id=(lax.rem(my + j, ny), mz), device_id_type=MESH,
        )
        copy.start()
        y_copies.append(copy)

    for copy in f_copies:
        copy.wait()

    edge_y = yf_y[...].astype(F32)
    edge_d = yf_d[...].astype(F32)

    def widen_field(x, _):
        stores = []
        for z in range(3):
            m = fb[x, pl.ds(64 * z, 32), :].astype(F32)
            source, at = (edge_y, 64 * z) if z < 2 else (edge_d, 0)
            last = pltpu.roll(source, 127 - at - x, 1)
            moved = jnp.where(lane == 127, last, pltpu.roll(m, 127, 1))
            stores.append((fb, (x, pl.ds(64 * z + 32, 32)), moved.astype(BF16)))
        return 0, stores

    in_blocks(nx + 1, widen_field, 0)

    def forward(xs, _):
        d = dot(w_fwd, jnp.concatenate([fb[pl.ds(x, 2)].reshape(384, 128) for x in xs], axis=1))
        stores = []
        for k, x in enumerate(xs):
            for half in range(2):
                for o in range(3):
                    at = 24 * half + 8 * o
                    row = pl.multiple_of(o * 8 * nx + x * 8, 8)
                    value = d[at:at + 8, 128 * k:128 * k + 128] + b_ref[o]
                    stores.append((des, (pl.ds(row, 8), pl.ds(128 * half, 128)), value))
        return 0, stores

    in_blocks(nx, forward, 0, 2)

    d_ref[...] = dot(des[...].astype(BF16), join).astype(BF16)

    for copy in y_copies:
        copy.wait()
    total = yrecv[0]
    for j in range(1, ny):
        total = total + yrecv[j]
    total = total * scale
    for o in range(3):
        gw_ref[o] = (total if o == 0 else pltpu.roll(total, 128 - 32 * o, 1))[0:27, 0:32]
        gb_ref[o] = jnp.sum(jnp.where(lane[0:1] == 96 + o, total[0:1], 0.0))


def body(ny, nz, field, weight, bias, cotangent):
    channels, planes, depth, width = field.shape
    nx = planes - 1
    cells = 8 * nx * depth * width * ny * nz
    forward, backward = selectors()
    fine = cotangent.shape
    vmem = pl.BlockSpec(memory_space=pltpu.VMEM)
    smem = pl.BlockSpec(memory_space=pltpu.SMEM)
    n_f, n_c = channels * planes * depth, fine[0] * fine[1] * fine[2]
    d, gi, gw, gb = pl.pallas_call(
        functools.partial(kernel, ny, nz, nx, 1.0 / math.sqrt(cells)),
        out_shape=(
            jax.ShapeDtypeStruct((n_c, fine[3]), BF16),
            jax.ShapeDtypeStruct((n_f, width), BF16),
            jax.ShapeDtypeStruct(weight.shape, F32),
            jax.ShapeDtypeStruct(bias.shape, F32),
        ),
        in_specs=[vmem, vmem, smem, vmem, vmem, vmem],
        out_specs=(vmem, vmem, vmem, smem),
        scratch_shapes=[
            pltpu.VMEM((n_f, 128), F32),
            pltpu.VMEM((nx + 1, 192, 128), BF16),
            pltpu.VMEM((32, 128), BF16),
            pltpu.VMEM((32, 128), BF16),
            pltpu.VMEM((32, 128), BF16),
            pltpu.VMEM((n_c, 256), F32),
            pltpu.VMEM((nx, 16, 128), BF16),
            pltpu.VMEM((nx, 16, 128), BF16),
            pltpu.VMEM((32, 128), BF16),
            pltpu.VMEM((32, 128), BF16),
            pltpu.VMEM((32, 128), BF16),
            pltpu.VMEM((nx + 2, 96, 128), BF16),
            pltpu.VMEM((n_f, 128), F32),
            pltpu.VMEM((n_c, 256), F32),
            pltpu.VMEM((96, 128), F32),
            pltpu.VMEM((32, 128), F32),
            pltpu.VMEM((32, 128), F32),
            pltpu.VMEM((nz, 32, 128), F32),
            pltpu.VMEM((ny, 32, 128), F32),
            pltpu.SemaphoreType.DMA((6,)),
            pltpu.SemaphoreType.DMA((6,)),
            pltpu.SemaphoreType.DMA((nz - 1,)),
            pltpu.SemaphoreType.DMA((nz - 1,)),
            pltpu.SemaphoreType.DMA((ny - 1,)),
            pltpu.SemaphoreType.DMA((ny - 1,)),
        ],
        compiler_params=pltpu.CompilerParams(
            collective_id=0, has_side_effects=True, vmem_limit_bytes=32 * 1024 * 1024
        ),
    )(
        field.reshape(n_f, width), weight, bias, cotangent.reshape(n_c, fine[3]),
        jnp.asarray(forward, BF16), jnp.asarray(backward, BF16),
    )
    return d.reshape(fine), gi.reshape(field.shape), gw, gb


def solution(mesh):
    return jax.shard_map(
        functools.partial(body, mesh.shape["gy"], mesh.shape["gz"]),
        mesh=mesh,
        in_specs=(P(None, None, "gz", "gy"), P(), P(), P(None, None, "gz", "gy")),
        out_specs=(P(None, None, "gz", "gy"), P(None, None, "gz", "gy"), P(), P()),
        check_vma=False,
    )
```

```python
import functools
import math

import jax
import jax.numpy as jnp
import numpy as np
from jax import lax
from jax.experimental import pallas as pl
from jax.experimental.pallas import tpu as pltpu
from jax.sharding import PartitionSpec as P

MESH = pl.DeviceIdType.MESH
F32 = jnp.float32
BF16 = jnp.bfloat16
NT = (((1,), (1,)), ((), ()))
LINK = {1: (0, 0), 2: (1, 0), 0: (1, 1)}


def selectors():
    forward = np.zeros((3, 48, 384), np.float32)
    backward = np.zeros((2, 96, 192), np.float32)
    for o in range(3):
        for t in range(27):
            (px, dx), (py, dy), (pz, dz) = LINK[t // 9], LINK[t // 3 % 3], LINK[t % 3]
            for z in range(2):
                block = dx * 6 + (z + dz) * 2 + dy
                row = py * 24 + o * 8 + px * 4 + z * 2 + pz
                forward[block // 4, row, block % 4 * 96 + o * 32 + t] = 1
                below = z - dz
                line = o * 8 + px * 4 + below * 2 + pz if below >= 0 else 24 + (3 + 4 * px + o) % 8
                backward[z, o * 32 + t, (1 - dx) * 96 + (py + dy) * 32 + line] = 1
    return forward, backward


def dot(a, b):
    return jnp.dot(a, b, preferred_element_type=F32)


def in_blocks(count, step, carry, wide=1, most=11):
    size = max(k for k in range(1, most + 1) if count % k == 0)

    def block(i, carry):
        stores = []
        for k in range(0, size, wide):
            xs = [i * size + j for j in range(k, min(k + wide, size))]
            carry, more = step(xs if wide > 1 else xs[0], carry)
            stores += more
        for ref, index, value in stores:
            ref[index] = value
        return carry

    return lax.fori_loop(0, count // size, block, carry)


def kernel(
    ny, nz, nx, scale,
    f_ref, w_ref, b_ref, c_ref, self_ref, selg_ref,
    d_ref, gi_ref, sum_ref,
    f32s, fb, yf, yf_y, yf_d, eo, hs, hr, yc, yc_y, yc_d, cb, gis, des, wp,
    part, pair, both, zsum, zrecv, yrecv,
    send_sem, recv_sem, zsend, zrsem, ysend, yrsem,
):
    my, mz = lax.axis_index("gy"), lax.axis_index("gz")
    y_up, y_dn = lax.rem(my + 1, ny), lax.rem(my + ny - 1, ny)
    z_up, z_dn = lax.rem(mz + 1, nz), lax.rem(mz + nz - 1, nz)
    rows = 2 * (nx + 1)

    barrier = pltpu.get_barrier_semaphore()
    for other in [z_up, z_dn] + [lax.rem(mz + 2 * j, nz) for j in range(1, nz // 2)]:
        pl.semaphore_signal(barrier, inc=1, device_id=(my, other), device_id_type=MESH)
    for j in range(1, ny):
        pl.semaphore_signal(barrier, inc=1, device_id=(lax.rem(my + j, ny), mz), device_id_type=MESH)
    pl.semaphore_signal(barrier, inc=1, device_id=(y_up, z_up), device_id_type=MESH)
    pl.semaphore_signal(barrier, inc=1, device_id=(y_dn, z_dn), device_id_type=MESH)

    lane = lax.broadcasted_iota(jnp.int32, (32, 128), 1)
    sub = lax.broadcasted_iota(jnp.int32, (8, 128), 0) % 4

    def send(k, src, dst, device):
        copy = pltpu.make_async_remote_copy(
            src_ref=src, dst_ref=dst, send_sem=send_sem.at[k], recv_sem=recv_sem.at[k],
            device_id=device, device_id_type=MESH,
        )
        copy.start()
        return copy

    i0 = lax.broadcasted_iota(jnp.int32, (256, 256), 0)
    i1 = lax.broadcasted_iota(jnp.int32, (256, 256), 1)
    split = jnp.where(i0 == 2 * (i1 % 128) + i1 // 128, 1.0, 0.0).astype(BF16)
    join = jnp.where(i1 == 2 * (i0 % 128) + i0 // 128, 1.0, 0.0).astype(BF16)
    eo[...] = dot(c_ref[...], split)

    def parts_of(x, half):
        return [
            eo[pl.ds(pl.multiple_of(o * 8 * nx + x * 8, 8), 8), 128 * half:128 * half + 128]
            for o in range(3)
        ]

    def last_z(p):
        top = jnp.where(sub == 3, p[0], 0.0)
        top = jnp.where(sub == 0, pltpu.roll(p[1], 1, 0), top)
        return jnp.where(sub == 1, pltpu.roll(p[2], 2, 0), top)

    def cot_step(x, carry):
        column, sums = carry
        even, odd = parts_of(x, 0), parts_of(x, 1)
        h_even, h_odd = last_z(even), last_z(odd)
        halo = jnp.concatenate([h_even, h_odd], axis=0).astype(BF16)
        m = jnp.concatenate(odd + [h_odd], axis=0)
        column = jnp.where(lane == x, m[:, 127:128], column)
        sums = [s + e + q for s, e, q in zip(sums, even, odd)]
        return (column, sums), [(hs, x, halo)]

    zero8 = jnp.zeros((8, 128), F32)
    column, sums = in_blocks(
        nx, cot_step, (jnp.zeros((32, 128), F32), [zero8, zero8, zero8])
    )
    yc[...] = column.astype(BF16)
    pl.semaphore_wait(barrier, 2 + nz // 2 - 1 + ny - 1 + 2)

    c_copies = [
        send(3, hs, hr, (my, z_up)),
        send(4, yc, yc_y, (y_up, mz)),
        send(5, yc, yc_d, (y_up, z_up)),
    ]

    f32s[...] = f_ref[...].astype(F32)

    def field_step(x, column):
        stores = []
        for z in range(2):
            m = f32s[pl.ds(2 * x + z, 32, stride=rows), :]
            stores.append((fb, (x, pl.ds(64 * z, 32)), m.astype(BF16)))
            column = jnp.where(lane == 64 * z + x, m[:, 0:1], column)
        return column, stores

    yf[...] = in_blocks(nx + 1, field_step, jnp.zeros((32, 128), F32)).astype(BF16)

    f_copies = [
        send(0, fb.at[:, pl.ds(0, 32), :], fb.at[:, pl.ds(128, 32), :], (my, z_dn)),
        send(1, yf, yf_y, (y_dn, mz)),
        send(2, yf, yf_d, (y_dn, z_dn)),
    ]

    wp[...] = jnp.zeros_like(wp)
    for o in range(3):
        wp[32 * o:32 * o + 27, 0:32] = w_ref[o].astype(F32)
    wv = wp[...]
    wt = wv + pltpu.roll(wv, 32, 1) + pltpu.roll(wv, 64, 1) + pltpu.roll(wv, 96, 1)
    lane96 = lax.broadcasted_iota(jnp.int32, (96, 128), 1) // 32
    stacked = jnp.concatenate([jnp.where(lane96 == g, wt, 0.0) for g in range(4)], axis=0).astype(BF16)
    w_fwd = jnp.concatenate([dot(self_ref[j], stacked) for j in range(3)], axis=1).astype(BF16)
    w_t = wv.T[0:32].astype(BF16)
    w_bwd = jnp.concatenate([dot(w_t, selg_ref[z]) for z in range(2)], axis=0).astype(BF16)

    for copy in c_copies:
        copy.wait()

    cb[0] = jnp.zeros((96, 128), BF16)
    cb[nx + 1] = jnp.zeros((96, 128), BF16)
    edge = jnp.concatenate([yc_y[...].astype(F32)[0:24], yc_d[...].astype(F32)[24:32]], axis=0)

    def widen_cot(x, _):
        below = hr[x].astype(F32)
        even = jnp.concatenate(parts_of(x, 0) + [below[0:8]], axis=0)
        odd = jnp.concatenate(parts_of(x, 1) + [below[8:16]], axis=0)
        first = pltpu.roll(edge, 128 - x, 1)
        moved = jnp.where(lane == 0, first, pltpu.roll(odd, 1, 1))
        return 0, [(cb, x + 1, jnp.concatenate([even, odd, moved], axis=0).astype(BF16))]

    in_blocks(nx, widen_cot, 0)

    def weight_step(xs, acc):
        taps = jnp.concatenate([cb[pl.ds(x, 2)].reshape(192, 128) for x in xs], axis=1)
        cells = jnp.concatenate([
            jnp.concatenate([fb[x, pl.ds(0, 32), :], fb[x, pl.ds(64, 32), :]], axis=0) for x in xs
        ], axis=1)
        return acc + lax.dot_general(cells, taps, NT, preferred_element_type=F32), []

    acc = in_blocks(nx + 1, weight_step, jnp.zeros((64, 192), F32), 2)
    acc = jnp.concatenate([acc, acc], axis=0)
    hi = acc.astype(BF16)
    lo = (acc - hi.astype(F32)).astype(BF16)
    v0, v1 = [
        lax.dot_general(selg_ref[z], hi, NT, preferred_element_type=F32)
        + lax.dot_general(selg_ref[z], lo, NT, preferred_element_type=F32)
        for z in range(2)
    ]
    g = v0 + pltpu.roll(v1, 96, 1)
    packed = jnp.where(
        lane < 32, g[0:32],
        jnp.where(lane < 64, pltpu.roll(g[32:64], 32, 1), pltpu.roll(g[64:96], 64, 1)),
    )
    for o in range(3):
        packed = jnp.where(lane == 96 + o, jnp.sum(sums[o]), packed)
    part[...] = packed
    pair_copy = send(6, part, pair, (my, mz + 1 - 2 * lax.rem(mz, 2)))

    def backward(xs, _):
        taps = jnp.concatenate([cb[pl.ds(x, 2)].reshape(192, 128) for x in xs], axis=1)
        g = dot(w_bwd, taps)
        return 0, [
            (gis, pl.ds(2 * x + z, 32, stride=rows), g[32 * z:32 * z + 32, 128 * k:128 * k + 128])
            for k, x in enumerate(xs) for z in range(2)
        ]

    in_blocks(nx + 1, backward, 0, 2)
    pair_copy.wait()
    chip = mz // 2
    both[...] = part[...] + pair[...]
    zrecv[chip] = both[...]
    z_copies = []
    for j in range(1, nz // 2):
        copy = pltpu.make_async_remote_copy(
            src_ref=both, dst_ref=zrecv.at[chip], send_sem=zsend.at[j - 1], recv_sem=zrsem.at[j - 1],
            device_id=(my, lax.rem(mz + 2 * j, nz)), device_id_type=MESH,
        )
        copy.start()
        z_copies.append(copy)

    gi_ref[...] = gis[...].astype(BF16)

    for copy in f_copies:
        copy.wait()

    edge_y = yf_y[...].astype(F32)
    edge_d = yf_d[...].astype(F32)

    def widen_field(x, _):
        stores = []
        for z in range(3):
            m = fb[x, pl.ds(64 * z, 32), :].astype(F32)
            source, at = (edge_y, 64 * z) if z < 2 else (edge_d, 0)
            last = pltpu.roll(source, 127 - at - x, 1)
            moved = jnp.where(lane == 127, last, pltpu.roll(m, 127, 1))
            stores.append((fb, (x, pl.ds(64 * z + 32, 32)), moved.astype(BF16)))
        return 0, stores

    in_blocks(nx + 1, widen_field, 0)

    for copy in z_copies:
        copy.wait()
    total = zrecv[0]
    for j in range(1, nz // 2):
        total = total + zrecv[j]
    zsum[...] = total
    yrecv[my] = total
    y_copies = []
    for j in range(1, ny):
        copy = pltpu.make_async_remote_copy(
            src_ref=zsum, dst_ref=yrecv.at[my], send_sem=ysend.at[j - 1], recv_sem=yrsem.at[j - 1],
            device_id=(lax.rem(my + j, ny), mz), device_id_type=MESH,
        )
        copy.start()
        y_copies.append(copy)

    def forward(xs, _):
        d = dot(w_fwd, jnp.concatenate([fb[pl.ds(x, 2)].reshape(384, 128) for x in xs], axis=1))
        stores = []
        for k, x in enumerate(xs):
            for half in range(2):
                for o in range(3):
                    at = 24 * half + 8 * o
                    row = pl.multiple_of(o * 8 * nx + x * 8, 8)
                    value = d[at:at + 8, 128 * k:128 * k + 128] + b_ref[o]
                    stores.append((des, (pl.ds(row, 8), pl.ds(128 * half, 128)), value))
        return 0, stores

    in_blocks(nx, forward, 0, 2)

    d_ref[...] = dot(des[...].astype(BF16), join).astype(BF16)

    for copy in y_copies:
        copy.wait()
    total = yrecv[0]
    for j in range(1, ny):
        total = total + yrecv[j]
    sum_ref[...] = total * scale


def finish(gi_in, sum_ref, gi_ref, gw_ref, gb_ref, sem):
    copy = pltpu.make_async_copy(gi_in, gi_ref, sem)
    copy.start()
    total = sum_ref[...]
    lane = lax.broadcasted_iota(jnp.int32, (1, 128), 1)
    for o in range(3):
        gw_ref[o] = (total if o == 0 else pltpu.roll(total, 128 - 32 * o, 1))[0:27, 0:32]
        gb_ref[o] = jnp.sum(jnp.where(lane == 96 + o, total[0:1], 0.0))
    copy.wait()


def body(ny, nz, field, weight, bias, cotangent):
    channels, planes, depth, width = field.shape
    nx = planes - 1
    cells = 8 * nx * depth * width * ny * nz
    forward, backward = selectors()
    fine = cotangent.shape
    vmem = pl.BlockSpec(memory_space=pltpu.VMEM)
    smem = pl.BlockSpec(memory_space=pltpu.SMEM)
    n_f, n_c = channels * planes * depth, fine[0] * fine[1] * fine[2]
    d, gi, total = pl.pallas_call(
        functools.partial(kernel, ny, nz, nx, 1.0 / math.sqrt(cells)),
        out_shape=(
            jax.ShapeDtypeStruct((n_c, fine[3]), BF16),
            jax.ShapeDtypeStruct((n_f, width), BF16),
            jax.ShapeDtypeStruct((32, 128), F32),
        ),
        in_specs=[vmem, vmem, smem, vmem, vmem, vmem],
        out_specs=(vmem, vmem, vmem),
        scratch_shapes=[
            pltpu.VMEM((n_f, 128), F32),
            pltpu.VMEM((nx + 1, 192, 128), BF16),
            pltpu.VMEM((32, 128), BF16),
            pltpu.VMEM((32, 128), BF16),
            pltpu.VMEM((32, 128), BF16),
            pltpu.VMEM((n_c, 256), F32),
            pltpu.VMEM((nx, 16, 128), BF16),
            pltpu.VMEM((nx, 16, 128), BF16),
            pltpu.VMEM((32, 128), BF16),
            pltpu.VMEM((32, 128), BF16),
            pltpu.VMEM((32, 128), BF16),
            pltpu.VMEM((nx + 2, 96, 128), BF16),
            pltpu.VMEM((n_f, 128), F32),
            pltpu.VMEM((n_c, 256), F32),
            pltpu.VMEM((96, 128), F32),
            pltpu.VMEM((32, 128), F32),
            pltpu.VMEM((32, 128), F32),
            pltpu.VMEM((32, 128), F32),
            pltpu.VMEM((32, 128), F32),
            pltpu.VMEM((nz // 2, 32, 128), F32),
            pltpu.VMEM((ny, 32, 128), F32),
            pltpu.SemaphoreType.DMA((7,)),
            pltpu.SemaphoreType.DMA((7,)),
            pltpu.SemaphoreType.DMA((max(1, nz // 2 - 1),)),
            pltpu.SemaphoreType.DMA((max(1, nz // 2 - 1),)),
            pltpu.SemaphoreType.DMA((ny - 1,)),
            pltpu.SemaphoreType.DMA((ny - 1,)),
        ],
        compiler_params=pltpu.CompilerParams(
            collective_id=0, has_side_effects=True, vmem_limit_bytes=32 * 1024 * 1024
        ),
    )(
        field.reshape(n_f, width), weight, bias, cotangent.reshape(n_c, fine[3]),
        jnp.asarray(forward, BF16), jnp.asarray(backward, BF16),
    )
    gi, gw, gb = pl.pallas_call(
        finish,
        out_shape=(
            jax.ShapeDtypeStruct(gi.shape, BF16),
            jax.ShapeDtypeStruct(weight.shape, F32),
            jax.ShapeDtypeStruct(bias.shape, F32),
        ),
        in_specs=[vmem, vmem],
        out_specs=(pl.BlockSpec(memory_space=pl.ANY), vmem, smem),
        scratch_shapes=[pltpu.SemaphoreType.DMA],
    )(gi, total)
    return d.reshape(fine), gi.reshape(field.shape), gw, gb


def solution(mesh):
    return jax.shard_map(
        functools.partial(body, mesh.shape["gy"], mesh.shape["gz"]),
        mesh=mesh,
        in_specs=(P(None, None, "gz", "gy"), P(), P(), P(None, None, "gz", "gy")),
        out_specs=(P(None, None, "gz", "gy"), P(None, None, "gz", "gy"), P(), P()),
        check_vma=False,
    )
```

```python
import functools
import math

import jax
import jax.numpy as jnp
import numpy as np
from jax import lax
from jax.experimental import pallas as pl
from jax.experimental.pallas import tpu as pltpu
from jax.sharding import PartitionSpec as P

MESH = pl.DeviceIdType.MESH
F32 = jnp.float32
BF16 = jnp.bfloat16
NT = (((1,), (1,)), ((), ()))
LINK = {1: (0, 0), 2: (1, 0), 0: (1, 1)}


def selectors():
    forward = np.zeros((3, 48, 384), np.float32)
    backward = np.zeros((2, 96, 192), np.float32)
    for o in range(3):
        for t in range(27):
            (px, dx), (py, dy), (pz, dz) = LINK[t // 9], LINK[t // 3 % 3], LINK[t % 3]
            for z in range(2):
                block = dx * 6 + (z + dz) * 2 + dy
                row = py * 24 + o * 8 + px * 4 + z * 2 + pz
                forward[block // 4, row, block % 4 * 96 + o * 32 + t] = 1
                below = z - dz
                line = o * 8 + px * 4 + below * 2 + pz if below >= 0 else 24 + (3 + 4 * px + o) % 8
                backward[z, o * 32 + t, (1 - dx) * 96 + (py + dy) * 32 + line] = 1
    return forward, backward


def dot(a, b):
    return jnp.dot(a, b, preferred_element_type=F32)


def in_blocks(count, step, carry, wide=1, most=11):
    size = max(k for k in range(1, most + 1) if count % k == 0)

    def block(i, carry):
        stores = []
        for k in range(0, size, wide):
            xs = [i * size + j for j in range(k, min(k + wide, size))]
            carry, more = step(xs if wide > 1 else xs[0], carry)
            stores += more
        for ref, index, value in stores:
            ref[index] = value
        return carry

    return lax.fori_loop(0, count // size, block, carry)


def kernel(
    ny, nz, nx, scale,
    f_ref, w_ref, b_ref, c_ref, self_ref, selg_ref,
    d_ref, gi_ref, gw_ref, gb_ref,
    f32s, fb, yf, yf_y, yf_d, eo, hs, hr, yc, yc_y, yc_d, cb, gis, des, wp,
    part, zsum, zrecv, yrecv,
    send_sem, recv_sem, zsend, zrsem, ysend, yrsem,
):
    my, mz = lax.axis_index("gy"), lax.axis_index("gz")
    y_up, y_dn = lax.rem(my + 1, ny), lax.rem(my + ny - 1, ny)
    z_up, z_dn = lax.rem(mz + 1, nz), lax.rem(mz + nz - 1, nz)
    rows = 2 * (nx + 1)

    barrier = pltpu.get_barrier_semaphore()
    for j in range(1, nz):
        pl.semaphore_signal(barrier, inc=1, device_id=(my, lax.rem(mz + j, nz)), device_id_type=MESH)
    for j in range(1, ny):
        pl.semaphore_signal(barrier, inc=1, device_id=(lax.rem(my + j, ny), mz), device_id_type=MESH)
    pl.semaphore_signal(barrier, inc=1, device_id=(y_up, z_up), device_id_type=MESH)
    pl.semaphore_signal(barrier, inc=1, device_id=(y_dn, z_dn), device_id_type=MESH)

    lane = lax.broadcasted_iota(jnp.int32, (32, 128), 1)
    sub = lax.broadcasted_iota(jnp.int32, (8, 128), 0) % 4

    def send(k, src, dst, device):
        copy = pltpu.make_async_remote_copy(
            src_ref=src, dst_ref=dst, send_sem=send_sem.at[k], recv_sem=recv_sem.at[k],
            device_id=device, device_id_type=MESH,
        )
        copy.start()
        return copy

    i0 = lax.broadcasted_iota(jnp.int32, (256, 256), 0)
    i1 = lax.broadcasted_iota(jnp.int32, (256, 256), 1)
    split = jnp.where(i0 == 2 * (i1 % 128) + i1 // 128, 1.0, 0.0).astype(BF16)
    join = jnp.where(i1 == 2 * (i0 % 128) + i0 // 128, 1.0, 0.0).astype(BF16)
    eo[...] = dot(c_ref[...], split)

    def parts_of(x, half):
        return [
            eo[pl.ds(pl.multiple_of(o * 8 * nx + x * 8, 8), 8), 128 * half:128 * half + 128]
            for o in range(3)
        ]

    def last_z(p):
        top = jnp.where(sub == 3, p[0], 0.0)
        top = jnp.where(sub == 0, pltpu.roll(p[1], 1, 0), top)
        return jnp.where(sub == 1, pltpu.roll(p[2], 2, 0), top)

    def cot_step(x, carry):
        column, sums = carry
        even, odd = parts_of(x, 0), parts_of(x, 1)
        h_even, h_odd = last_z(even), last_z(odd)
        halo = jnp.concatenate([h_even, h_odd], axis=0).astype(BF16)
        m = jnp.concatenate(odd + [h_odd], axis=0)
        column = jnp.where(lane == x, m[:, 127:128], column)
        sums = [s + e + q for s, e, q in zip(sums, even, odd)]
        return (column, sums), [(hs, x, halo)]

    zero8 = jnp.zeros((8, 128), F32)
    column, sums = in_blocks(
        nx, cot_step, (jnp.zeros((32, 128), F32), [zero8, zero8, zero8])
    )
    yc[...] = column.astype(BF16)
    pl.semaphore_wait(barrier, nz - 1 + ny - 1 + 2)

    c_copies = [
        send(3, hs, hr, (my, z_up)),
        send(4, yc, yc_y, (y_up, mz)),
        send(5, yc, yc_d, (y_up, z_up)),
    ]

    f32s[...] = f_ref[...].astype(F32)

    def field_step(x, column):
        stores = []
        for z in range(2):
            m = f32s[pl.ds(2 * x + z, 32, stride=rows), :]
            stores.append((fb, (x, pl.ds(64 * z, 32)), m.astype(BF16)))
            column = jnp.where(lane == 64 * z + x, m[:, 0:1], column)
        return column, stores

    yf[...] = in_blocks(nx + 1, field_step, jnp.zeros((32, 128), F32)).astype(BF16)

    f_copies = [
        send(0, fb.at[:, pl.ds(0, 32), :], fb.at[:, pl.ds(128, 32), :], (my, z_dn)),
        send(1, yf, yf_y, (y_dn, mz)),
        send(2, yf, yf_d, (y_dn, z_dn)),
    ]

    wp[...] = jnp.zeros_like(wp)
    for o in range(3):
        wp[32 * o:32 * o + 27, 0:32] = w_ref[o].astype(F32)
    wv = wp[...]
    wt = wv + pltpu.roll(wv, 32, 1) + pltpu.roll(wv, 64, 1) + pltpu.roll(wv, 96, 1)
    lane96 = lax.broadcasted_iota(jnp.int32, (96, 128), 1) // 32
    stacked = jnp.concatenate([jnp.where(lane96 == g, wt, 0.0) for g in range(4)], axis=0).astype(BF16)
    w_fwd = jnp.concatenate([dot(self_ref[j], stacked) for j in range(3)], axis=1).astype(BF16)
    w_t = wv.T[0:32].astype(BF16)
    w_bwd = jnp.concatenate([dot(w_t, selg_ref[z]) for z in range(2)], axis=0).astype(BF16)

    for copy in c_copies:
        copy.wait()

    cb[0] = jnp.zeros((96, 128), BF16)
    cb[nx + 1] = jnp.zeros((96, 128), BF16)
    edge = jnp.concatenate([yc_y[...].astype(F32)[0:24], yc_d[...].astype(F32)[24:32]], axis=0)

    def widen_cot(x, _):
        below = hr[x].astype(F32)
        even = jnp.concatenate(parts_of(x, 0) + [below[0:8]], axis=0)
        odd = jnp.concatenate(parts_of(x, 1) + [below[8:16]], axis=0)
        first = pltpu.roll(edge, 128 - x, 1)
        moved = jnp.where(lane == 0, first, pltpu.roll(odd, 1, 1))
        return 0, [(cb, x + 1, jnp.concatenate([even, odd, moved], axis=0).astype(BF16))]

    in_blocks(nx, widen_cot, 0)

    def weight_step(xs, acc):
        taps = jnp.concatenate([cb[pl.ds(x, 2)].reshape(192, 128) for x in xs], axis=1)
        cells = jnp.concatenate([
            jnp.concatenate([fb[x, pl.ds(0, 32), :], fb[x, pl.ds(64, 32), :]], axis=0) for x in xs
        ], axis=1)
        return acc + lax.dot_general(cells, taps, NT, preferred_element_type=F32), []

    acc = in_blocks(nx + 1, weight_step, jnp.zeros((64, 192), F32), 2)
    acc = jnp.concatenate([acc, acc], axis=0)
    hi = acc.astype(BF16)
    lo = (acc - hi.astype(F32)).astype(BF16)
    v0, v1 = [
        lax.dot_general(selg_ref[z], hi, NT, preferred_element_type=F32)
        + lax.dot_general(selg_ref[z], lo, NT, preferred_element_type=F32)
        for z in range(2)
    ]
    g = v0 + pltpu.roll(v1, 96, 1)
    packed = jnp.where(
        lane < 32, g[0:32],
        jnp.where(lane < 64, pltpu.roll(g[32:64], 32, 1), pltpu.roll(g[64:96], 64, 1)),
    )
    for o in range(3):
        packed = jnp.where(lane == 96 + o, jnp.sum(sums[o]), packed)
    part[...] = packed
    zrecv[mz] = packed
    z_copies = []
    for j in range(1, nz):
        copy = pltpu.make_async_remote_copy(
            src_ref=part, dst_ref=zrecv.at[mz], send_sem=zsend.at[j - 1], recv_sem=zrsem.at[j - 1],
            device_id=(my, lax.rem(mz + j, nz)), device_id_type=MESH,
        )
        copy.start()
        z_copies.append(copy)

    def backward(xs, _):
        taps = jnp.concatenate([cb[pl.ds(x, 2)].reshape(192, 128) for x in xs], axis=1)
        g = dot(w_bwd, taps)
        return 0, [
            (gis, pl.ds(2 * x + z, 32, stride=rows), g[32 * z:32 * z + 32, 128 * k:128 * k + 128])
            for k, x in enumerate(xs) for z in range(2)
        ]

    in_blocks(nx + 1, backward, 0, 2)
    gi_ref[...] = gis[...].astype(BF16)

    f_copies[1].wait()
    edge_y = yf_y[...].astype(F32)

    def widen_field(edge, planes, x, _):
        stores = []
        for z in planes:
            m = fb[x, pl.ds(64 * z, 32), :].astype(F32)
            last = pltpu.roll(edge, 127 - 64 * (z % 2) - x, 1)
            moved = jnp.where(lane == 127, last, pltpu.roll(m, 127, 1))
            stores.append((fb, (x, pl.ds(64 * z + 32, 32)), moved.astype(BF16)))
        return 0, stores

    in_blocks(nx + 1, functools.partial(widen_field, edge_y, (0, 1)), 0)

    for copy in z_copies:
        copy.wait()
    total = zrecv[0]
    for j in range(1, nz):
        total = total + zrecv[j]
    zsum[...] = total
    yrecv[my] = total
    y_copies = []
    for j in range(1, ny):
        copy = pltpu.make_async_remote_copy(
            src_ref=zsum, dst_ref=yrecv.at[my], send_sem=ysend.at[j - 1], recv_sem=yrsem.at[j - 1],
            device_id=(lax.rem(my + j, ny), mz), device_id_type=MESH,
        )
        copy.start()
        y_copies.append(copy)

    f_copies[0].wait()
    f_copies[2].wait()
    edge_d = yf_d[...].astype(F32)
    in_blocks(nx + 1, functools.partial(widen_field, edge_d, (2,)), 0)

    def forward(xs, _):
        d = dot(w_fwd, jnp.concatenate([fb[pl.ds(x, 2)].reshape(384, 128) for x in xs], axis=1))
        stores = []
        for k, x in enumerate(xs):
            for half in range(2):
                for o in range(3):
                    at = 24 * half + 8 * o
                    row = pl.multiple_of(o * 8 * nx + x * 8, 8)
                    value = d[at:at + 8, 128 * k:128 * k + 128] + b_ref[o]
                    stores.append((des, (pl.ds(row, 8), pl.ds(128 * half, 128)), value))
        return 0, stores

    in_blocks(nx, forward, 0, 2)

    d_ref[...] = dot(des[...].astype(BF16), join).astype(BF16)

    for copy in y_copies:
        copy.wait()
    total = yrecv[0]
    for j in range(1, ny):
        total = total + yrecv[j]
    total = total * scale
    for o in range(3):
        gw_ref[o] = (total if o == 0 else pltpu.roll(total, 128 - 32 * o, 1))[0:27, 0:32]
        gb_ref[o] = jnp.sum(jnp.where(lane[0:1] == 96 + o, total[0:1], 0.0))


def body(ny, nz, field, weight, bias, cotangent):
    channels, planes, depth, width = field.shape
    nx = planes - 1
    cells = 8 * nx * depth * width * ny * nz
    forward, backward = selectors()
    fine = cotangent.shape
    vmem = pl.BlockSpec(memory_space=pltpu.VMEM)
    smem = pl.BlockSpec(memory_space=pltpu.SMEM)
    n_f, n_c = channels * planes * depth, fine[0] * fine[1] * fine[2]
    d, gi, gw, gb = pl.pallas_call(
        functools.partial(kernel, ny, nz, nx, 1.0 / math.sqrt(cells)),
        out_shape=(
            jax.ShapeDtypeStruct((n_c, fine[3]), BF16),
            jax.ShapeDtypeStruct((n_f, width), BF16),
            jax.ShapeDtypeStruct(weight.shape, F32),
            jax.ShapeDtypeStruct(bias.shape, F32),
        ),
        in_specs=[vmem, vmem, smem, vmem, vmem, vmem],
        out_specs=(vmem, vmem, vmem, smem),
        scratch_shapes=[
            pltpu.VMEM((n_f, 128), F32),
            pltpu.VMEM((nx + 1, 192, 128), BF16),
            pltpu.VMEM((32, 128), BF16),
            pltpu.VMEM((32, 128), BF16),
            pltpu.VMEM((32, 128), BF16),
            pltpu.VMEM((n_c, 256), F32),
            pltpu.VMEM((nx, 16, 128), BF16),
            pltpu.VMEM((nx, 16, 128), BF16),
            pltpu.VMEM((32, 128), BF16),
            pltpu.VMEM((32, 128), BF16),
            pltpu.VMEM((32, 128), BF16),
            pltpu.VMEM((nx + 2, 96, 128), BF16),
            pltpu.VMEM((n_f, 128), F32),
            pltpu.VMEM((n_c, 256), F32),
            pltpu.VMEM((96, 128), F32),
            pltpu.VMEM((32, 128), F32),
            pltpu.VMEM((32, 128), F32),
            pltpu.VMEM((nz, 32, 128), F32),
            pltpu.VMEM((ny, 32, 128), F32),
            pltpu.SemaphoreType.DMA((6,)),
            pltpu.SemaphoreType.DMA((6,)),
            pltpu.SemaphoreType.DMA((nz - 1,)),
            pltpu.SemaphoreType.DMA((nz - 1,)),
            pltpu.SemaphoreType.DMA((ny - 1,)),
            pltpu.SemaphoreType.DMA((ny - 1,)),
        ],
        compiler_params=pltpu.CompilerParams(
            collective_id=0, has_side_effects=True, vmem_limit_bytes=32 * 1024 * 1024
        ),
    )(
        field.reshape(n_f, width), weight, bias, cotangent.reshape(n_c, fine[3]),
        jnp.asarray(forward, BF16), jnp.asarray(backward, BF16),
    )
    return d.reshape(fine), gi.reshape(field.shape), gw, gb


def solution(mesh):
    return jax.shard_map(
        functools.partial(body, mesh.shape["gy"], mesh.shape["gz"]),
        mesh=mesh,
        in_specs=(P(None, None, "gz", "gy"), P(), P(), P(None, None, "gz", "gy")),
        out_specs=(P(None, None, "gz", "gy"), P(None, None, "gz", "gy"), P(), P()),
        check_vma=False,
    )
```
